256 devices in a mesh: dp: 8 (over y, x_hi), seq: 16 (over z, core), cell: 2 (over x_lo).
Axes of the slice: x: 4 (x_hi: 2, x_lo: 2; x = x_hi * 2 + x_lo), y: 4, z: 8, core: 2. Of those that a mesh axis runs over, the one named last changes fastest.
Arguments:
- cells: bfloat16 [8, 16384, 768], P('dp', ('seq', 'cell')), may hold values from -64 to 64
- anchor_ids: int32 [8, 16384], P('dp', ('seq', 'cell')), may hold values from 0 to 511, as said below
- cell_counts: int32 [8, 32], P('dp', ('seq', 'cell')), may hold values from 384 to 512, as said below
- anchor_gain: float32 [768], replicated, may hold values from 0.5 to 1.5
- w_query: bfloat16 [768, 768], replicated, may hold values from -0.21875 to 0.21875
- w_keyval: bfloat16 [768, 1536], replicated, may hold values from -0.21875 to 0.21875
- w_out: bfloat16 [768, 768], replicated, may hold values from -0.21875 to 0.21875
- cotangent: bfloat16 [8, 16384, 768], P('dp', ('seq', 'cell')), may hold values from -6 to 6
Outputs:
- cell_update: bfloat16 [8, 16384, 768], P('dp', ('seq', 'cell'))
- grad_query: float32 [768, 768], P(('seq', 'cell'))
- grad_keyval: float32 [768, 1536], P(('seq', 'cell'))
- grad_out: float32 [768, 768], P(('seq', 'cell'))
The draws below stay inside these ranges and needn't reach their ends.
Inputs may be any that keep to these rules, and one draw needn't show every extreme that they name: `anchor_ids`: anchors o * 16 to (o + 1) * 16 - 1 belong to owner o of the sample. The valid cells of one device name anchors of any one owner at most 32 times, and each device's first 32 cells all name anchors of its own index. `cell_counts`: in every sample some device has all 512 cells valid.
All inputs are finite; a program needn't handle non-finite values.
Results may differ from the reference program's by a relative error of at most 0.035.
The reference program's roundings to bfloat16 on the way count: a program that leaves them out, or rounds other values in their place, can miss the bound.
Values may be sent and summed in bfloat16 or wider, within the bound.
A program may use at most 128 MiB of HBM per device.

```python
import math
import jax
import jax.numpy as jnp
from jax import lax

D = 768
HEADS = 12
HEAD = 64
CELL_DEV = 512
A_DEV = 16
SAMPLES = 8
OWNERS = 32
CELLS = 16384
ANCHORS = 512
CAP = 32


def draw_cells(key, part):
    key = jax.random.fold_in(key, 11)
    key_one = jax.random.fold_in(key, 0)
    values_out = jax.random.normal(key_one, (SAMPLES, CELLS, D), jnp.float32)
    return jnp.clip(values_out, -64.0, 64.0).astype(jnp.bfloat16)


def draw_anchor_ids(key, part):
    key = jax.random.fold_in(key, 23)
    key_one, key_two = jax.random.split(key)
    device = jnp.arange(OWNERS, dtype=jnp.int32)[None, :, None]
    row_index = jnp.arange(CELL_DEV, dtype=jnp.int32)[None, None, :]
    group_index = row_index // CAP
    coin_flip = jax.random.randint(key_one, (SAMPLES, OWNERS, CELL_DEV), 0, 2).astype(jnp.int32)
    offset = jnp.where(group_index == 0, 0, 2 * group_index - coin_flip)
    owner_of = (device + offset) % OWNERS
    local_id = jax.random.randint(key_two, (SAMPLES, OWNERS, CELL_DEV), 0, A_DEV)
    return (owner_of * A_DEV + local_id).reshape(SAMPLES, CELLS).astype(jnp.int32)


def draw_cell_counts(key, part):
    key = jax.random.fold_in(key, 37)
    key_one, key_two = jax.random.split(key)
    counts = jax.random.randint(key_one, (SAMPLES, OWNERS), 3 * CELL_DEV // 4, CELL_DEV + 1)
    chosen = jax.random.randint(key_two, (SAMPLES, 1), 0, OWNERS)
    return jnp.where(jnp.arange(OWNERS, dtype=jnp.int32)[None, :] == chosen, CELL_DEV, counts).astype(jnp.int32)


def steps_of(rng, dims, cuts, smallest, largest):
    factor_of, own = 1.0, jax.random.fold_in(rng, 6)
    for axis_at, parts in cuts:
        draws = jnp.exp(jax.random.uniform(jax.random.fold_in(own, axis_at), (parts,), jnp.float32, smallest / len(cuts), largest / len(cuts)))
        factor_of = factor_of * jnp.repeat(draws, dims[axis_at] // parts).reshape([-1 if axis == axis_at else 1 for axis in range(len(dims))])
    return factor_of


def scatter_about(rng, dims, width, limit, cuts=(), kind=jnp.bfloat16):
    entries = jax.random.normal(rng, dims, jnp.float32) * width
    if len(cuts) > 0:
        entries = steps_of(rng, dims, cuts, -0.22, 0.18) * entries
    return jnp.clip(entries, min=-limit, max=limit).astype(kind)


def setup_inputs(seed: int = 0) -> dict:
    key_list = jax.random.split(jax.random.key(seed), 9)
    return {
        "cells": draw_cells(jax.random.fold_in(key_list[8], 71), 0),
        "anchor_ids": draw_anchor_ids(jax.random.fold_in(key_list[8], 71), 0),
        "cell_counts": draw_cell_counts(jax.random.fold_in(key_list[8], 71), 0),
        "anchor_gain": jnp.clip(1.0 + 0.1 * jax.random.normal(key_list[3], (D,), jnp.float32), 0.5, 1.5),
        "w_query": scatter_about(key_list[4], (D, D), D ** -0.5, 0.21875),
        "w_keyval": scatter_about(key_list[5], (D, 2 * D), D ** -0.5, 0.21875),
        "w_out": scatter_about(key_list[6], (D, D), D ** -0.5, 0.21875),
        "cotangent": scatter_about(key_list[7], (SAMPLES, CELLS, D), 1.0, 6.0, ((0, 8), (1, 32))),
    }


def split_heads(matrix):
    return matrix.reshape(matrix.shape[0], HEADS, HEAD).astype(jnp.float32)

def lowered(values_in):
    return lax.optimization_barrier(values_in.astype(jnp.bfloat16)).astype(jnp.float32)

def reference(cells, anchor_ids, cell_counts, anchor_gain, w_query, w_keyval, w_out, cotangent):
    score_scale = 1.0 / math.sqrt(HEAD)
    positions = jnp.arange(CELLS, dtype=jnp.int32)
    anchor_range = jnp.arange(ANCHORS, dtype=jnp.int32)
    grad_query = jnp.zeros((D, D), jnp.float32)
    grad_keyval = jnp.zeros((D, 2 * D), jnp.float32)
    grad_out = jnp.zeros((D, D), jnp.float32)
    updates = []
    for sample in range(SAMPLES):
        cell_rows = cells[sample]
        row_limit = jnp.repeat(cell_counts[sample], CELL_DEV)
        is_valid = (positions % CELL_DEV < row_limit).astype(jnp.float32)
        membership = (anchor_ids[sample][None, :] == anchor_range[:, None]).astype(jnp.float32) * is_valid[None, :]
        pooled_sum = jnp.dot(membership, cell_rows.astype(jnp.float32), precision=lax.Precision.HIGHEST)
        anchor_count = lax.optimization_barrier(jnp.sum(membership, axis=1))
        pooled = pooled_sum / jnp.maximum(anchor_count, 1.0)[:, None]
        normed = (pooled * lax.rsqrt(lax.optimization_barrier(jnp.mean(pooled * pooled, axis=1)) + 1e-06)[:, None] * anchor_gain).astype(jnp.bfloat16)
        keyval = jnp.dot(normed, w_keyval, preferred_element_type=jnp.float32).astype(jnp.bfloat16)
        key_heads = split_heads(keyval[:, :D])
        value_heads = split_heads(keyval[:, D:])
        queries = jnp.dot(cell_rows, w_query, preferred_element_type=jnp.float32).astype(jnp.bfloat16)
        query_blocks = queries.reshape(OWNERS, CELL_DEV, D)

        def forward_block(q_block):
            logits = jnp.einsum('chd,ahd->hca', split_heads(q_block), key_heads) * score_scale
            row_peak = lax.optimization_barrier(jnp.max(logits, axis=2))
            exp_terms = jnp.exp(logits - row_peak[:, :, None])
            row_total = lax.optimization_barrier(jnp.sum(exp_terms, axis=2))
            head_mix = jnp.einsum('hca,ahd->hcd', lowered(exp_terms), value_heads) / row_total[:, :, None]
            flat_mix = jnp.transpose(head_mix, (1, 0, 2)).reshape(CELL_DEV, D).astype(jnp.bfloat16)
            return (flat_mix, row_peak, row_total)
        attended, row_peaks, totals = lax.map(forward_block, query_blocks)
        attended = attended.reshape(CELLS, D)
        cell_delta = jnp.dot(attended, w_out, preferred_element_type=jnp.float32) * is_valid[:, None]
        updates.append(cell_delta.astype(jnp.bfloat16))
        masked = cotangent[sample] * is_valid[:, None].astype(jnp.bfloat16)
        grad_out = grad_out + jnp.dot(attended.T, masked, preferred_element_type=jnp.float32)
        d_attended = jnp.dot(masked, w_out.T, preferred_element_type=jnp.float32).astype(jnp.bfloat16)
        row_delta = lax.optimization_barrier(jnp.sum(split_heads(d_attended) * split_heads(attended), axis=2))
        delta_blocks = jnp.transpose(row_delta.reshape(OWNERS, CELL_DEV, HEADS), (0, 2, 1))

        def backward_block(run_state, inputs):
            d_key, d_value = run_state
            q_block, d_block, row_peak, row_total, block_delta = inputs
            q_heads = split_heads(q_block)
            d_heads = split_heads(d_block)
            logits = jnp.einsum('chd,ahd->hca', q_heads, key_heads) * score_scale
            attn_prob = jnp.exp(logits - row_peak[:, :, None]) / row_total[:, :, None]
            d_prob = jnp.einsum('chd,ahd->hca', d_heads, value_heads)
            d_logits = lowered(attn_prob * (d_prob - block_delta[:, :, None]) * score_scale)
            prob_low = lowered(attn_prob)
            d_query = jnp.einsum('hca,ahd->chd', d_logits, key_heads).reshape(CELL_DEV, D).astype(jnp.bfloat16)
            d_key = d_key + jnp.einsum('hca,chd->ahd', d_logits, q_heads)
            d_value = d_value + jnp.einsum('hca,chd->ahd', prob_low, d_heads)
            return ((d_key, d_value), d_query)
        zero_heads = jnp.zeros((ANCHORS, HEADS, HEAD), jnp.float32)
        (d_key, d_value), d_query = lax.scan(backward_block, (zero_heads, zero_heads), (query_blocks, d_attended.reshape(OWNERS, CELL_DEV, D), row_peaks, totals, delta_blocks))
        d_query = d_query.reshape(CELLS, D)
        grad_query = grad_query + jnp.dot(cell_rows.T, d_query, preferred_element_type=jnp.float32)
        key_terms = jnp.concatenate([d_key.reshape(ANCHORS, D), d_value.reshape(ANCHORS, D)], axis=1)
        grad_keyval = grad_keyval + jnp.dot(normed.astype(jnp.float32).T, key_terms, precision=lax.Precision.HIGHEST)
    return (jnp.stack(updates), grad_query, grad_keyval, grad_out)
```

```python
import functools
import math

import jax
import jax.numpy as jnp
from jax import lax
from jax.experimental import pallas as pl
from jax.experimental.pallas import tpu as pltpu
from jax.sharding import PartitionSpec as P

HEADS = 12
HEAD = 64
A_DEV = 16
D = 768
ROWS = 512
WIDE = D + 128
CHUNKS = 4
UNIT = (48, 384)
F32 = jnp.float32
BF16 = jnp.bfloat16
MESH = pl.DeviceIdType.MESH


def place():
    dp, seq, xl = lax.axis_index("dp"), lax.axis_index("seq"), lax.axis_index("cell")
    return dp, seq // 2, seq % 2, xl


def remote(src, dst, send, recv, device):
    return pltpu.make_async_remote_copy(
        src_ref=src, dst_ref=dst, send_sem=send, recv_sem=recv, device_id=device, device_id_type=MESH
    )


def greet(peers):
    barrier = pltpu.get_barrier_semaphore()
    for peer in peers:
        pl.semaphore_signal(barrier, inc=1, device_id=peer, device_id_type=MESH)
    pl.semaphore_wait(barrier, len(peers))


def sample_peers(dp, z, c, xl):
    return [
        (dp, lax.rem(z + dz, 8) * 2 + c, lax.rem(xl + dx, 2))
        for dz in (4, 3, 5, 2, 6, 1, 7, 0)
        for dx in (1, 0)
        if (dz, dx) != (0, 0)
    ]


PEER_STEPS = [(dz, dx) for dz in (4, 3, 5, 2, 6, 1, 7, 0) for dx in (1, 0) if (dz, dx) != (0, 0)]


def pool_kernel(
    count_ref, ids_ref, cells_ref, gain_ref, out_ref,
    core_out, core_in, own, sent, got, every,
    core_send, core_recv, peer_send, peer_recv, spread_send, spread_recv, twin_send, twin_recv,
):
    dp, z, c, xl = place()
    twin = (dp, z * 2 + 1 - c, xl)
    peers = sample_peers(dp, z, c, xl)
    greet([twin] + peers)
    ids = ids_ref[...]
    valid = lax.broadcasted_iota(jnp.int32, (1, ROWS), 1) < count_ref[0, 0]
    ids = jnp.where(valid, ids, -1)
    row = lax.broadcasted_iota(jnp.int32, (256, ROWS), 0)
    base = (row // 32) * 64 + row % 32

    def partial_sums(core):
        hot = jnp.where(ids == base + core * 32, 1.0, 0.0).astype(BF16)
        sums = jnp.dot(hot, cells_ref[...], preferred_element_type=F32)
        counts = jnp.dot(hot, jnp.ones((ROWS, 128), BF16), preferred_element_type=F32)
        return sums, counts

    sums, counts = partial_sums(1 - c)
    core_out[:, :D] = sums.astype(BF16)
    core_out[:, D:] = counts.astype(BF16)
    first = remote(core_out, core_in, core_send, core_recv, twin)
    first.start()
    sums, counts = partial_sums(c)
    own[:, :D] = sums
    own[:, D:] = counts
    first.wait_recv()
    own[...] += core_in[...].astype(F32)
    sent[...] = own[...].astype(BF16).reshape(16, 16, WIDE)
    copies = []
    for at, ((dz, dx), peer) in enumerate(zip(PEER_STEPS, peers)):
        there = lax.rem(z + dz, 8) * 2 + lax.rem(xl + dx, 2)
        copy = remote(sent.at[there], got.at[at], peer_send.at[at], peer_recv.at[at], peer)
        copy.start()
        copies.append(copy)
    me = z * 2 + xl
    total = own[pl.ds(pl.multiple_of(me * 16, 16), 16), :]
    for at in reversed(range(15)):
        copies[at].wait_recv()
        total = total + got[at].astype(F32)
    pooled = total[:, :D] / jnp.maximum(total[:, D : D + 1], 1.0)
    scale = lax.rsqrt(jnp.mean(pooled * pooled, axis=1, keepdims=True) + 1e-06)
    every[c, me] = (pooled * scale * gain_ref[...]).astype(BF16)
    spreads = []
    for at, peer in enumerate(peers):
        copy = remote(every.at[c, me], every.at[c, me], spread_send.at[at], spread_recv.at[at], peer)
        copy.start()
        spreads.append(copy)
    twins = []
    for at in [15] + list(reversed(range(15))):
        if at == 15:
            here = me
        else:
            dz, dx = PEER_STEPS[at]
            here = lax.rem(z + 8 - dz, 8) * 2 + lax.rem(xl + dx, 2)
            remote(
                every.at[c, here], every.at[c, here], spread_send.at[at], spread_recv.at[at], peers[at]
            ).wait_recv()
        copy = remote(every.at[c, here], every.at[c, here], twin_send.at[at], twin_recv.at[at], twin)
        copy.start()
        twins.append(copy)
    for copy in twins:
        copy.wait_recv()
    out_ref[...] = every[...]
    first.wait_send()
    for copy in copies + spreads + twins:
        copy.wait_send()


def pool(count, ids, cells, gain):
    vmem = pl.BlockSpec(memory_space=pltpu.VMEM)
    dma = pltpu.SemaphoreType.DMA
    return pl.pallas_call(
        pool_kernel,
        out_shape=jax.ShapeDtypeStruct((2, 16, A_DEV, D), BF16),
        in_specs=[pl.BlockSpec(memory_space=pltpu.SMEM), vmem, vmem, vmem],
        out_specs=vmem,
        scratch_shapes=[
            pltpu.VMEM((256, WIDE), BF16),
            pltpu.VMEM((256, WIDE), BF16),
            pltpu.VMEM((256, WIDE), F32),
            pltpu.VMEM((16, 16, WIDE), BF16),
            pltpu.VMEM((15, 16, WIDE), BF16),
            pltpu.VMEM((2, 16, A_DEV, D), BF16),
            dma, dma, dma((15,)), dma((15,)), dma((15,)), dma((15,)), dma((16,)), dma((16,)),
        ],
        compiler_params=pltpu.CompilerParams(
            collective_id=0, has_side_effects=True, vmem_limit_bytes=32 * 1024 * 1024
        ),
        cost_estimate=pl.CostEstimate(flops=10**9, bytes_accessed=4 * 10**6, transcendentals=0),
    )(count, ids, cells, gain)


def reduce_kernel(
    g_ref, out_ref, twin_in, first_out, first_in, second_out, second_in, root_out, root_in, last,
    twin_send, twin_recv, first_send, first_recv, second_send, second_recv,
    root_send, root_recv, last_send, last_recv,
):
    dp, z, c, xl = place()
    y, xh = dp // 2, dp % 2
    x = xh * 2 + xl
    seq = z * 2 + c
    twin = (dp, z * 2 + 1 - c, xl)
    my_first = jnp.where(c == 0, x, y)
    my_second = jnp.where(c == 0, y, x)

    def along_x(to):
        return (y * 2 + to // 2, seq, lax.rem(to, 2))

    def along_y(to):
        return (to * 2 + xh, seq, xl)

    def choose(to, is_x):
        a, b = along_x(to), along_y(to)
        return tuple(jnp.where(is_x, i, j) for i, j in zip(a, b))

    def step(at, j):
        return lax.rem(at + j, 4)

    firsts = [choose(step(my_first, j), c == 0) for j in (1, 2, 3)]
    seconds = [choose(step(my_second, j), c == 1) for j in (1, 2, 3)]
    others = [(lax.rem(dp + j, 8), seq, xl) for j in range(1, 8)]
    greet(
        [twin]
        + [along_x(step(x, j)) for j in (1, 2, 3)]
        + [along_y(step(y, j)) for j in (1, 2, 3)]
        + [(step(y, j) * 2 + 1 - xh, seq, xl) for j in (1, 2, 3)]
        + [(dp, lax.rem(z + j, 8) * 2 + c, xl) for j in range(1, 8)]
    )
    sends = []

    def twin_copy(k):
        return remote(g_ref.at[k, 1 - c], twin_in.at[k], twin_send.at[k], twin_recv.at[k], twin)

    def first_copy(k, j):
        to = step(my_first, j)
        return remote(
            first_out.at[k, to], first_in.at[k, j - 1], first_send.at[k, j - 1], first_recv.at[k, j - 1],
            firsts[j - 1],
        )

    def second_copy(k, j):
        to = step(my_second, j)
        return remote(
            second_out.at[k, to], second_in.at[k, j - 1], second_send.at[k, j - 1],
            second_recv.at[k, j - 1], seconds[j - 1],
        )

    root = (dp, dp * 2 + c, xl)
    is_root = z == dp

    def last_copy(k, j):
        return remote(last.at[k], last.at[k], last_send.at[k, j - 1], last_recv.at[k], others[j - 1])

    def stage0(k):
        twin_copy(k).start()

    def stage1(k):
        twin_copy(k).wait_recv()

        def unit(u, _):
            to = jnp.where(c == 0, (u % 4) * 4 + u // 4, u)
            both = g_ref[k, c, u].astype(F32) + twin_in[k, u].astype(F32)
            first_out[k, to // 4, to % 4] = both.astype(BF16)
            return 0

        lax.fori_loop(0, 16, unit, 0)
        for j in (2, 1, 3):
            first_copy(k, j).start()

    def stage2(k):
        for j in (1, 3, 2):
            first_copy(k, j).wait_recv()

        def unit(b, _):
            total = first_out[k, my_first, b].astype(F32)
            for j in range(3):
                total = total + first_in[k, j, b].astype(F32)
            second_out[k, b] = total.astype(BF16)
            return 0

        lax.fori_loop(0, 4, unit, 0)
        for j in (2, 1, 3):
            second_copy(k, j).start()

    def stage3(k):
        for j in (1, 3, 2):
            second_copy(k, j).wait_recv()
        total = second_out[k, my_second].astype(F32)
        for j in range(3):
            total = total + second_in[k, j].astype(F32)
        root_out[k] = total.astype(BF16)

        @pl.when(jnp.logical_not(is_root))
        def _():
            at = lax.rem(z - dp + 8, 8) - 1
            remote(root_out.at[k], root_in.at[k, at], root_send.at[k], root_recv.at[k, at], root).start()

    def stage4(k):
        @pl.when(is_root)
        def _():
            total = root_out[k].astype(F32)
            for j in range(7):
                remote(root_out.at[k], root_in.at[k, j], root_send.at[k], root_recv.at[k, j], twin).wait_recv()
                total = total + root_in[k, j].astype(F32)
            last[k] = total.astype(BF16)
            for j in range(1, 8):
                last_copy(k, j).start()

    def stage5(k):
        @pl.when(jnp.logical_not(is_root))
        def _():
            last_copy(k, 1).wait_recv()

        out_ref[k] = last[k].astype(F32)

    stages = [stage0, stage1, stage2, stage3, stage4, stage5]
    for tick in range(CHUNKS + len(stages) - 1):
        for s in reversed(range(len(stages))):
            if 0 <= tick - s < CHUNKS:
                stages[s](tick - s)

    for k in range(CHUNKS):
        twin_copy(k).wait_send()
        for j in (1, 2, 3):
            first_copy(k, j).wait_send()
            second_copy(k, j).wait_send()

        @pl.when(jnp.logical_not(is_root))
        def _():
            remote(root_out.at[k], root_in.at[k, 0], root_send.at[k], root_recv.at[k, 0], root).wait_send()

        @pl.when(is_root)
        def _():
            for j in range(1, 8):
                last_copy(k, j).wait_send()


def reduce_all(grads):
    vmem = pl.BlockSpec(memory_space=pltpu.VMEM)
    dma = pltpu.SemaphoreType.DMA
    return pl.pallas_call(
        reduce_kernel,
        out_shape=jax.ShapeDtypeStruct((CHUNKS, *UNIT), F32),
        in_specs=[vmem],
        out_specs=vmem,
        scratch_shapes=[
            pltpu.VMEM((CHUNKS, 16, *UNIT), BF16),
            pltpu.VMEM((CHUNKS, 4, 4, *UNIT), BF16),
            pltpu.VMEM((CHUNKS, 3, 4, *UNIT), BF16),
            pltpu.VMEM((CHUNKS, 4, *UNIT), BF16),
            pltpu.VMEM((CHUNKS, 3, *UNIT), BF16),
            pltpu.VMEM((CHUNKS, *UNIT), BF16),
            pltpu.VMEM((CHUNKS, 7, *UNIT), BF16),
            pltpu.VMEM((CHUNKS, *UNIT), BF16),
            dma((CHUNKS,)), dma((CHUNKS,)),
            dma((CHUNKS, 3)), dma((CHUNKS, 3)),
            dma((CHUNKS, 3)), dma((CHUNKS, 3)),
            dma((CHUNKS,)), dma((CHUNKS, 7)),
            dma((CHUNKS, 7)), dma((CHUNKS,)),
        ],
        compiler_params=pltpu.CompilerParams(
            collective_id=1, has_side_effects=True, vmem_limit_bytes=40 * 1024 * 1024
        ),
        cost_estimate=pl.CostEstimate(flops=10**7, bytes_accessed=5 * 10**6, transcendentals=0),
    )(grads)


def split_heads(matrix):
    return matrix.reshape(matrix.shape[0], HEADS, matrix.shape[1] // HEADS)


def shards(cells, anchor_ids, cell_counts, anchor_gain, w_query, w_keyval, w_out, cotangent):
    cell_rows = cells[0]
    n_rows = ROWS
    score_scale = 1.0 / math.sqrt(HEAD)
    valid_mask = jnp.arange(n_rows, dtype=jnp.int32) < cell_counts[0, 0]
    is_valid = valid_mask.astype(F32)
    normed = pool(cell_counts, anchor_ids, cell_rows, anchor_gain[None, :]).reshape(512, D)
    keyval = jnp.dot(normed, w_keyval, preferred_element_type=F32).astype(BF16)
    queries = jnp.dot(cell_rows, w_query, preferred_element_type=F32).astype(BF16)
    query_heads = split_heads(queries)
    key_heads = split_heads(keyval[:, :D])
    value_heads = split_heads(keyval[:, D:])
    logits = (
        jnp.einsum("chd,ahd->hca", query_heads, key_heads, preferred_element_type=F32) * score_scale
    )
    row_peak = jnp.max(logits, axis=2)
    exp_terms = jnp.exp(logits - row_peak[:, :, None])
    weighted = jnp.einsum(
        "hca,ahd->hcd", exp_terms.astype(BF16), value_heads, preferred_element_type=F32
    )
    row_total = jnp.sum(exp_terms, axis=2)
    attended = (
        jnp.transpose(weighted / row_total[:, :, None], (1, 0, 2)).reshape(n_rows, D).astype(BF16)
    )
    cell_delta = jnp.dot(attended, w_out, preferred_element_type=F32) * is_valid[:, None]
    cell_update = cell_delta.astype(BF16)[None]
    masked = cotangent[0] * valid_mask[:, None].astype(BF16)
    grad_out = jnp.einsum("cd,ce->de", attended, masked, preferred_element_type=F32)
    d_attended = jnp.einsum("ce,de->cd", masked, w_out, preferred_element_type=F32).astype(BF16)
    d_heads = split_heads(d_attended)
    row_delta = jnp.transpose(
        jnp.sum(d_heads.astype(F32) * split_heads(attended).astype(F32), axis=2)
    )
    attn_prob = exp_terms / row_total[:, :, None]
    d_prob = jnp.einsum("chd,ahd->hca", d_heads, value_heads, preferred_element_type=F32)
    d_logits = (attn_prob * (d_prob - row_delta[:, :, None]) * score_scale).astype(BF16)
    d_query = jnp.einsum("hca,ahd->chd", d_logits, key_heads, preferred_element_type=F32)
    d_key = jnp.einsum("hca,chd->ahd", d_logits, query_heads, preferred_element_type=F32)
    d_value = jnp.einsum(
        "hca,chd->ahd", attn_prob.astype(BF16), d_heads, preferred_element_type=F32
    )
    d_query = d_query.reshape(n_rows, D).astype(BF16)
    grad_query = jnp.einsum("cd,ce->de", cell_rows, d_query, preferred_element_type=F32)
    d_keyval = jnp.concatenate([d_key.reshape(512, D), d_value.reshape(512, D)], axis=1)
    grad_keyval = jnp.einsum("ad,ae->de", normed, d_keyval.astype(BF16), preferred_element_type=F32)
    chunks = [grad_out]
    for quad in range(3):
        cols = slice(quad * 256, quad * 256 + 256)
        vals = slice(D + quad * 256, D + quad * 256 + 256)
        chunks.append(
            jnp.concatenate([grad_query[:, cols], grad_keyval[:, cols], grad_keyval[:, vals]], axis=1)
        )
    grads = jnp.stack(chunks).astype(BF16).reshape(CHUNKS, 8, 2, 2, 24, 2, 384)
    grads = jnp.transpose(grads, (0, 2, 1, 3, 5, 4, 6)).reshape(CHUNKS, 2, 16, *UNIT)
    done = reduce_all(grads)
    done = jnp.concatenate([done[:, :24], done[:, 24:]], axis=2)
    return (
        cell_update,
        jnp.concatenate([done[1 + q, :, :256] for q in range(3)], axis=1),
        jnp.concatenate(
            [done[1 + q, :, 256:512] for q in range(3)] + [done[1 + q, :, 512:] for q in range(3)], axis=1
        ),
        done[0],
    )


def solution(mesh):
    return jax.shard_map(
        shards,
        mesh=mesh,
        in_specs=(
            P("dp", ("seq", "cell"), None),
            P("dp", ("seq", "cell")),
            P("dp", ("seq", "cell")),
            P(),
            P(),
            P(),
            P(),
            P("dp", ("seq", "cell"), None),
        ),
        out_specs=(
            P("dp", ("seq", "cell"), None),
            P(("seq", "cell"), None),
            P(("seq", "cell"), None),
            P(("seq", "cell"), None),
        ),
        check_vma=False,
    )
```
